256 devices in a mesh: dp: 256 (over z, y, x, core).
Axes of the slice: x: 4, y: 4, z: 8, core: 2. Of those that a mesh axis runs over, the one named last changes fastest.
Arguments:
- image_emb: bfloat16 [131072, 1152], P('dp'), may hold values from -0.19921875 to 0.19921875
- text_feat: bfloat16 [131072, 1152], P('dp'), may hold values from -6 to 6
- text_head: bfloat16 [1152, 1152], replicated, may hold values from -0.1875 to 0.1875
- pair_ids: int32 [131072], P('dp'), may hold values from 0 to 16383
- row_weight: bfloat16 [131072], P('dp'), as said below
Outputs:
- loss: float32 [1], replicated
- grad_image: bfloat16 [131072, 1152], P('dp')
- grad_text: bfloat16 [131072, 1152], P('dp')
- grad_head: bfloat16 [1152, 1152], replicated
The draws below stay inside these ranges and needn't reach their ends.
Inputs may be any that keep to these rules, and one draw needn't show every extreme that they name: Every row_weight is positive.
All inputs are finite; a program needn't handle non-finite values.
Results may differ from the reference program's by a relative error of at most 0.012.
Values may be sent and summed in bfloat16 or wider, within the bound.
A program may use at most 128 MiB of HBM per device.

```python
import jax
import jax.numpy as jnp
from jax import lax

E = 1152
D = 1152
ROWS = 512
TOKENS = 131072
N_DP = 256


def draw_row_weight(key, part):
    key = jax.random.fold_in(key, 7)
    blocks = TOKENS // ROWS
    place = (jnp.arange(TOKENS) // ROWS).astype(jnp.float32) / max(blocks - 1, 1)
    base = jnp.exp(jax.random.uniform(key, (TOKENS,), jnp.float32, -1.0, 1.0))
    ramp = 1.0 + 2.0 * place
    return (base * ramp).astype(jnp.bfloat16)


def touch_ends(result, own_key, least, top_value):
    index_at = [jax.random.randint(jax.random.fold_in(own_key, axis), (), 0, length) for axis, length in enumerate(result.shape)]
    widest = result.shape.index(max(result.shape))
    next_to = index_at[:widest] + [(index_at[widest] + 1) % result.shape[widest]] + index_at[widest + 1:]
    return result.at[tuple(index_at)].set(least).at[tuple(next_to)].set(top_value)


def steps_of(rng, dims, pieces, least, largest):
    def one(position, shards_of):
        heights = jax.random.uniform(jax.random.fold_in(jax.random.fold_in(rng, 6), position), (shards_of,), jnp.float32, least / len(pieces), largest / len(pieces))
        return jnp.repeat(jnp.exp(heights), dims[position] // shards_of).reshape((-1,) + (1,) * (len(dims) - position - 1))

    factor_of = one(*pieces[0])
    for cut in pieces[1:]:
        factor_of = factor_of * one(*cut)
    return factor_of


def normal_values(key, dims, deviation, bound, pieces=(), held_as=jnp.bfloat16):
    values = jax.random.normal(key, dims, jnp.float32) * deviation
    if len(pieces) > 0:
        values = steps_of(key, dims, pieces, -0.22, 0.18) * values
    return jnp.clip(values, min=-bound, max=bound).astype(held_as)


def setup_inputs(seed: int = 0) -> dict:
    seeds = jax.random.split(jax.random.key(seed), 6)
    image_emb = normal_values(seeds[0], (TOKENS, E), 0.03, 0.19921875, ((0, 256),))
    text_feat = normal_values(seeds[1], (TOKENS, D), 1.0, 6.0, ((0, 256),))
    text_head = normal_values(seeds[2], (D, E), D ** -0.5, 0.1875)
    pair_ids = touch_ends(jax.random.randint(seeds[3], (TOKENS,), 0, TOKENS // 8), jax.random.fold_in(seeds[3], 1), 0, (TOKENS // 8) - 1).astype(jnp.int32)
    row_weight = draw_row_weight(jax.random.fold_in(seeds[5], 71), 0)
    return dict(image_emb=image_emb, text_feat=text_feat, text_head=text_head, pair_ids=pair_ids, row_weight=row_weight)


logit_scale = 10.0
logit_bias = -2.0
norm_eps = 1e-06

def normalize(values):
    length = jnp.sqrt(lax.optimization_barrier(jnp.sum(values * values, axis=-1, keepdims=True)) + norm_eps)
    return (values / length, length)

def signal(zi_rows, ids_rows, weight_rows, zt_cols, ids_cols):
    logit = logit_scale * jnp.dot(zi_rows, zt_cols.T, preferred_element_type=jnp.float32) + logit_bias
    sign = jnp.where(ids_rows[:, None] == ids_cols[None, :], 1.0, -1.0).astype(jnp.float32)
    weight = weight_rows.astype(jnp.float32)[:, None]
    total = jnp.sum(weight * jax.nn.softplus(-sign * logit))
    dlog = (-sign * weight * jax.nn.sigmoid(-sign * logit)).astype(jnp.bfloat16)
    return (total, dlog)

def image_part(dlog, zt_cols):
    return logit_scale * jnp.dot(dlog, zt_cols, preferred_element_type=jnp.float32)

def text_part(dlog, zi_rows):
    product = lax.dot_general(dlog, zi_rows, (((0,), (0,)), ((), ())), preferred_element_type=jnp.float32)
    return (logit_scale * product).astype(jnp.bfloat16)

def reference(image_emb, text_feat, text_head, pair_ids, row_weight):
    count = N_DP
    rows = ROWS
    u = jnp.dot(text_feat, text_head, preferred_element_type=jnp.float32)
    zt32, text_len = normalize(u)
    zt = zt32.astype(jnp.bfloat16)
    zi32, image_len = normalize(image_emb.astype(jnp.float32))
    zi = zi32.astype(jnp.bfloat16)
    zi_blocks = zi.reshape(count, rows, -1)
    zt_blocks = zt.reshape(count, rows, -1)
    id_blocks = pair_ids.reshape(count, rows)
    weight_blocks = row_weight.reshape(count, rows)

    def per_block(block):
        partners = [block, jnp.bitwise_xor(block, count // 2), jnp.bitwise_xor(block, 1)]
        loss_sum = jnp.float32(0.0)
        grad_rows = jnp.zeros((rows, zi.shape[1]), jnp.float32)
        parts = []
        for other in partners:
            total, dlog = signal(zi_blocks[block], id_blocks[block], weight_blocks[block], zt_blocks[other], id_blocks[other])
            loss_sum = loss_sum + total
            grad_rows = grad_rows + image_part(dlog, zt_blocks[other])
            parts.append(text_part(dlog, zi_blocks[block]))
        return (loss_sum, grad_rows, jnp.stack(parts))
    blocks = jnp.arange(count, dtype=jnp.int32)
    losses, dzi_blocks, parts = lax.map(per_block, blocks)
    far_one = jnp.bitwise_xor(blocks, count // 2)
    far_two = jnp.bitwise_xor(blocks, 1)
    dzt_blocks = parts[:, 0].astype(jnp.float32) + parts[far_one, 1].astype(jnp.float32) + parts[far_two, 2].astype(jnp.float32)
    dzi = dzi_blocks.reshape(zi.shape)
    dzt = dzt_blocks.reshape(zt.shape)
    grad_image = ((dzi - zi32 * lax.optimization_barrier(jnp.sum(zi32 * dzi, axis=-1, keepdims=True))) / image_len).astype(jnp.bfloat16)
    du = ((dzt - zt32 * lax.optimization_barrier(jnp.sum(zt32 * dzt, axis=-1, keepdims=True))) / text_len).astype(jnp.bfloat16)
    grad_text = lax.dot_general(du, text_head, (((1,), (1,)), ((), ())), preferred_element_type=jnp.float32).astype(jnp.bfloat16)
    grad_head = lax.dot_general(text_feat, du, (((0,), (0,)), ((), ())), preferred_element_type=jnp.float32).astype(jnp.bfloat16)
    loss = (jnp.sum(losses) / (3.0 * rows * rows * count)).reshape(1)
    return (loss, grad_image, grad_text, grad_head)
```

```python
import functools

import jax
import jax.numpy as jnp
from jax import lax
from jax.experimental import pallas as pl
from jax.experimental.pallas import tpu as pltpu
from jax.sharding import PartitionSpec as P

MESH = pl.DeviceIdType.MESH
F32 = jnp.float32
BF16 = jnp.bfloat16

SCALE = 10.0
BIAS = -2.0
EPS = 1e-06

ROWS = 512
WIDTH = 1152
CHUNK = 128
CHUNKS = ROWS // CHUNK

UNITS = (WIDTH // 16) * (WIDTH // 128)
HALF = UNITS // 2
STREAM = HALF // 2
PIECE1 = 44
PIECE2 = 11
PIECE3 = 3


def dot_nt(a, b):
    return lax.dot_general(a, b, (((1,), (1,)), ((), ())), preferred_element_type=F32)


def dot_nn(a, b):
    return lax.dot_general(a, b, (((1,), (0,)), ((), ())), preferred_element_type=F32)


def dot_tn(a, b):
    return lax.dot_general(a, b, (((0,), (0,)), ((), ())), preferred_element_type=F32)


def rows_of(i, size=CHUNK):
    return pl.ds(pl.multiple_of(i * size, size), size)


def kernel(
    image_ref, text_ref, head_ref, ids_ref, weight_ref,
    loss_ref, gi_ref, gt_ref, gh_ref,
    image, text, head, zi, zi_inv, zt32, zt_inv, zt, zt_near, zt_far, text_far,
    ids_near, ids_far, dzt, dzi, part_near, got_near, part_far, got_far, du, du_far,
    dlog_own, dlog_near, dlog_far, loss_row, head_acc,
    units, got_a, half_b, got_b, sum_b, got_c, sum_c, got_d, gat_d, gat_c, gat_b, gat_a,
    loss_core, loss_x, loss_y, loss_z,
    load_sem, f_send, f_recv, id_send, id_recv, n_send, n_recv, np_send, np_recv, r_send, r_recv,
    a_send, a_recv, b_send, b_recv, c_send, c_recv, d_send, d_recv,
    e_send, e_recv, g_send, g_recv, h_send, h_recv, i_send, i_recv,
    l_send, l_recv, gate_sem,
):
    me = lax.axis_index("dp")
    core = me % 2
    x = (me // 2) % 4
    y = (me // 8) % 4
    z = me // 32

    def at(zz, yy, xx, cc):
        return ((zz * 4 + yy) * 4 + xx) * 2 + cc

    near = at(z, y, x, 1 - core)
    far = at((z + 4) % 8, y, x, core)

    def x_peer(d):
        return at(z, y, (x + d) % 4, core)

    def y_peer(d):
        return at(z, (y + d) % 4, x, core)

    def z_peer(d):
        return at((z + d) % 8, y, x, core)

    def remote(src, dst, send, recv, device):
        return pltpu.make_async_remote_copy(
            src_ref=src, dst_ref=dst, send_sem=send, recv_sem=recv,
            device_id=(device,), device_id_type=MESH,
        )

    loads = [
        pltpu.make_async_copy(head_ref, head, load_sem.at[0]),
        pltpu.make_async_copy(text_ref, text, load_sem.at[1]),
        pltpu.make_async_copy(image_ref, image, load_sem.at[2]),
    ]
    for load in loads:
        load.start()

    barrier = pltpu.get_barrier_semaphore()
    peers = [near] + [x_peer(d) for d in (1, 2, 3)] + [y_peer(d) for d in (1, 2, 3)] + [z_peer(d) for d in range(1, 8)]
    for peer in peers:
        pl.semaphore_signal(barrier, inc=1, device_id=(peer,), device_id_type=MESH)
    pl.semaphore_wait(barrier, len(peers))

    send_ids_far = remote(ids_ref, ids_far, id_send.at[0], id_recv.at[0], far)
    send_ids_near = remote(ids_ref, ids_near, id_send.at[1], id_recv.at[1], near)
    send_ids_far.start()
    send_ids_near.start()

    def forward(i):
        return remote(text_ref.at[rows_of(i)], text_far.at[rows_of(i)], f_send.at[i], f_recv.at[i], far)

    for i in range(CHUNKS):
        forward(i).start()

    loads[0].wait()
    loads[1].wait()

    def project(i, carry):
        rows = rows_of(i)
        u = dot_nn(text[rows, :], head[...])
        inv = 1.0 / jnp.sqrt(jnp.sum(u * u, axis=1, keepdims=True) + EPS)
        unit = u * inv
        zt32[rows, :] = unit
        zt_inv[rows, :] = inv
        zt[rows, :] = unit.astype(BF16)
        return carry

    lax.fori_loop(0, CHUNKS, project, 0)
    send_zt = remote(zt, zt_near, n_send, n_recv, near)
    send_zt.start()

    loads[2].wait()

    def image_norm(i, carry):
        rows = rows_of(i)
        v = image[rows, :].astype(F32)
        inv = 1.0 / jnp.sqrt(jnp.sum(v * v, axis=1, keepdims=True) + EPS)
        zi_inv[rows, :] = inv
        zi[rows, :] = (v * inv).astype(BF16)
        return carry

    lax.fori_loop(0, CHUNKS, image_norm, 0)

    own_ids = ids_ref[...]
    ids_image = jnp.concatenate([own_ids[i : i + 1, :] for i in range(CHUNKS)], axis=1)
    weight = weight_ref[...].astype(F32)
    loss_row[...] = jnp.zeros_like(loss_row)

    def tile(texts, ids_row):
        s = dot_nt(texts, zi[...])
        logit = SCALE * s + BIAS
        ids_col = jnp.transpose(jnp.broadcast_to(ids_row, (CHUNK, CHUNK)))[:, :1]
        same = ids_col == ids_image
        v = jnp.where(same, -logit, logit)
        e = jnp.exp(-jnp.abs(v))
        soft = jnp.maximum(v, 0.0) + jnp.log1p(e)
        loss_row[...] += jnp.sum(soft, axis=0, keepdims=True)
        sig = jnp.where(v >= 0.0, 1.0, e) / (1.0 + e)
        d = (jnp.where(same, -weight, weight) * sig).astype(BF16)
        part = (SCALE * dot_nn(d, zi[...])).astype(BF16)
        return d, part

    def own_tile(i, carry):
        rows = rows_of(i)
        d, part = tile(zt[rows, :], ids_ref[pl.ds(i, 1), :])
        dlog_own[rows, :] = d
        dzt[rows, :] = part.astype(F32)
        return carry

    lax.fori_loop(0, CHUNKS, own_tile, 0)

    send_ids_near.wait_recv()
    send_zt.wait_recv()

    def near_part(i):
        return remote(part_near.at[rows_of(i)], got_near.at[rows_of(i)], np_send.at[i], np_recv.at[i], near)

    def near_tile(i, carry):
        rows = rows_of(i)
        d, part = tile(zt_near[rows, :], ids_near[pl.ds(i, 1), :])
        dlog_near[rows, :] = d
        part_near[rows, :] = part
        near_part(i).start()
        return carry

    lax.fori_loop(0, CHUNKS, near_tile, 0)

    def image_grad(i, carry):
        cols = rows_of(i)
        dzi[cols, :] = dot_tn(dlog_own[:, cols], zt[...]) + dot_tn(dlog_near[:, cols], zt_near[...])
        return carry

    lax.fori_loop(0, CHUNKS, image_grad, 0)

    def own_du(i, carry):
        rows = rows_of(i)
        near_part(i).wait_recv()
        g = dzt[rows, :] + got_near[rows, :].astype(F32)
        dzt[rows, :] = g
        unit = zt32[rows, :]
        du[rows, :] = ((g - unit * jnp.sum(unit * g, axis=1, keepdims=True)) * zt_inv[rows, :]).astype(BF16)
        return carry

    lax.fori_loop(0, CHUNKS, own_du, 0)

    def head_own(i, carry):
        cols = rows_of(i)
        head_acc[cols, :] = dot_tn(text[:, cols], du[...])
        return carry

    lax.fori_loop(0, WIDTH // 128, head_own, 0)

    send_ids_far.wait_recv()

    def back(i):
        return remote(part_far.at[rows_of(i)], got_far.at[rows_of(i)], r_send.at[i], r_recv.at[i], far)

    def far_tile(i):
        rows = rows_of(i)
        u = dot_nn(text_far[rows, :], head[...])
        inv = 1.0 / jnp.sqrt(jnp.sum(u * u, axis=1, keepdims=True) + EPS)
        unit = u * inv
        texts = unit.astype(BF16)
        zt_far[rows, :] = texts
        d, part = tile(texts, ids_far[pl.ds(i, 1), :])
        dlog_far[rows, :] = d
        part_far[rows, :] = part
        g = part.astype(F32)
        du_far[rows, :] = ((g - unit * jnp.sum(unit * g, axis=1, keepdims=True)) * inv).astype(BF16)

    def far_step(i, carry):
        forward(i).wait_recv()

        @pl.when(i == CHUNKS - 1)
        def _():
            pl.semaphore_signal(gate_sem, inc=1, device_id=(z_peer(6),), device_id_type=MESH)
            pl.semaphore_wait(gate_sem, 1)
            for j in range(CHUNKS - 1):
                back(j).start()

        far_tile(i)
        return carry

    lax.fori_loop(0, CHUNKS, far_step, 0)
    back(CHUNKS - 1).start()

    def head_all(i, carry):
        cols = rows_of(i)
        total = head_acc[cols, :] + dot_tn(text_far[:, cols], du_far[...])
        out = total.astype(BF16)
        for r in range(8):
            for c in range(9):
                units[i * 72 + (r * 9 + c)] = out[16 * r : 16 * r + 16, 128 * c : 128 * c + 128]
        return carry

    lax.fori_loop(0, WIDTH // 128, head_all, 0)
    loss_core[core] = jnp.broadcast_to(jnp.sum(weight * loss_row[...]).reshape(1, 1), (8, 128))

    copy_a = remote(units.at[pl.ds((1 - core) * HALF, HALF)], got_a, a_send, a_recv, near)
    copy_a.start()
    loss_a = remote(loss_core.at[core], loss_core.at[core], l_send.at[0], l_recv.at[0], near)
    loss_a.start()

    def finish_image(i, carry):
        rows = rows_of(i)
        g = SCALE * (dzi[rows, :] + dot_tn(dlog_far[:, rows], zt_far[...]))
        inv = zi_inv[rows, :]
        unit = image[rows, :].astype(F32) * inv
        gi_ref[rows, :] = ((g - unit * jnp.sum(unit * g, axis=1, keepdims=True)) * inv).astype(BF16)
        return carry

    def finish_text(i):
        back(i).wait_recv()
        rows = rows_of(i)
        g = dzt[rows, :] + got_far[rows, :].astype(F32)
        unit = zt32[rows, :]
        d = ((g - unit * jnp.sum(unit * g, axis=1, keepdims=True)) * zt_inv[rows, :]).astype(BF16)
        gt_ref[rows, :] = dot_nt(d, head[...]).astype(BF16)

    copy_a.wait_recv()
    loss_a.wait_recv()
    loss_x[x] = loss_core[0] + loss_core[1]

    def add_a(i, carry):
        own = units[pl.ds(core * HALF + i * 12, 12)].astype(F32)
        half_b[pl.ds(i * 12, 12)] = (own + got_a[pl.ds(i * 12, 12)].astype(F32)).astype(BF16)
        return carry

    lax.fori_loop(0, HALF // 12, add_a, 0)
    half_b[pl.ds(HALF, 16)] = jnp.zeros((16, 16, 128), BF16)

    first = [(x_peer, x), (y_peer, y)]
    second = [(y_peer, y), (x_peer, x)]
    copies_b = []
    for s in range(2):
        peer, at_s = first[s]
        for d in (1, 2, 3):
            to = (at_s + d) % 4
            k = 3 * s + d - 1
            copies_b.append(remote(half_b.at[pl.ds(STREAM * s + PIECE1 * to, PIECE1)], got_b.at[k], b_send.at[k], b_recv.at[k], peer(d)))
    loss_b = [remote(loss_x.at[x], loss_x.at[x], l_send.at[d], l_recv.at[d], x_peer(d)) for d in (1, 2, 3)]
    for copy in copies_b + loss_b:
        copy.start()

    lax.fori_loop(0, CHUNKS, finish_image, 0)

    for copy in copies_b + loss_b:
        copy.wait_recv()
    loss_y[y] = (loss_x[0] + loss_x[1]) + (loss_x[2] + loss_x[3])
    for s in range(2):
        base = STREAM * s + PIECE1 * first[s][1]

        def add_b(i, carry, s=s, base=base):
            total = half_b[pl.ds(base + i * 11, 11)].astype(F32)
            for k in range(3 * s, 3 * s + 3):
                total = total + got_b[k, pl.ds(i * 11, 11)].astype(F32)
            sum_b[s, pl.ds(i * 11, 11)] = total.astype(BF16)
            return carry

        lax.fori_loop(0, 4, add_b, 0)

    copies_c = []
    for s in range(2):
        peer, at_s = second[s]
        for d in (1, 2, 3):
            to = (at_s + d) % 4
            k = 3 * s + d - 1
            copies_c.append(remote(sum_b.at[s, pl.ds(PIECE2 * to, PIECE2)], got_c.at[k], c_send.at[k], c_recv.at[k], peer(d)))
    loss_c = [remote(loss_y.at[y], loss_y.at[y], l_send.at[3 + d], l_recv.at[3 + d], y_peer(d)) for d in (1, 2, 3)]
    for copy in copies_c + loss_c:
        copy.start()
    for copy in copies_c + loss_c:
        copy.wait_recv()
    loss_z[z] = (loss_y[0] + loss_y[1]) + (loss_y[2] + loss_y[3])
    for s in range(2):
        total = sum_b[s, pl.ds(PIECE2 * second[s][1], PIECE2)].astype(F32)
        for k in range(3 * s, 3 * s + 3):
            total = total + got_c[k].astype(F32)
        sum_c[pl.ds(PIECE2 * s, PIECE2)] = total.astype(BF16)
    sum_c[pl.ds(2 * PIECE2, 2)] = jnp.zeros((2, 16, 128), BF16)

    copies_d = []
    for d in range(1, 8):
        to = (z + d) % 8
        copies_d.append(remote(sum_c.at[pl.ds(PIECE3 * to, PIECE3)], got_d.at[d - 1], d_send.at[d - 1], d_recv.at[d - 1], z_peer(d)))
    loss_d = [remote(loss_z.at[z], loss_z.at[z], l_send.at[6 + d], l_recv.at[6 + d], z_peer(d)) for d in range(1, 8)]
    for copy in copies_d + loss_d:
        copy.start()
    for copy in copies_d + loss_d:
        copy.wait_recv()
    total = sum_c[pl.ds(PIECE3 * z, PIECE3)].astype(F32)
    for k in range(7):
        total = total + got_d[k].astype(F32)
    gat_d[pl.ds(PIECE3 * z, PIECE3)] = total.astype(BF16)
    sums = [loss_z[k] for k in range(8)]
    loss_all = ((sums[0] + sums[1]) + (sums[2] + sums[3])) + ((sums[4] + sums[5]) + (sums[6] + sums[7]))
    loss_ref[0] = jnp.max(loss_all) / (3.0 * ROWS * ROWS * 256)

    mine = gat_d.at[pl.ds(PIECE3 * z, PIECE3)]
    copies_e = [remote(mine, mine, e_send.at[d - 1], e_recv.at[d - 1], z_peer(d)) for d in range(1, 8)]
    for copy in copies_e:
        copy.start()
    finish_text(0)
    for copy in copies_e:
        copy.wait_recv()

    copies_g = []
    for s in range(2):
        peer, at_s = second[s]
        src = gat_d.at[pl.ds(PIECE2 * s, PIECE2)]
        dst = gat_c.at[s, pl.ds(PIECE2 * at_s, PIECE2)]
        for d in (1, 2, 3):
            k = 3 * s + d - 1
            copies_g.append(remote(src, dst, g_send.at[k], g_recv.at[k], peer(d)))
    for copy in copies_g:
        copy.start()
    for s in range(2):
        gat_c[s, pl.ds(PIECE2 * second[s][1], PIECE2)] = gat_d[pl.ds(PIECE2 * s, PIECE2)]
    for copy in copies_g:
        copy.wait_recv()

    copies_h = []
    for s in range(2):
        peer, at_s = first[s]
        dst = gat_b.at[s, pl.ds(PIECE1 * at_s, PIECE1)]
        for d in (1, 2, 3):
            k = 3 * s + d - 1
            copies_h.append(remote(gat_c.at[s], dst, h_send.at[k], h_recv.at[k], peer(d)))
    for copy in copies_h:
        copy.start()
    for s in range(2):
        gat_b[s, pl.ds(PIECE1 * first[s][1], PIECE1)] = gat_c[s]
    finish_text(1)
    for copy in copies_h:
        copy.wait_recv()

    copy_i = remote(gat_b, gat_a, i_send, i_recv, near)
    copy_i.start()

    def write_head(src, which):
        for s in range(2):

            def body(r, carry, s=s):
                row = pl.ds(pl.multiple_of(which * (HALF // 9 * 16) + s * (STREAM // 9 * 16) + r * 16, 16), 16)
                for c in range(9):
                    gh_ref[row, 128 * c : 128 * c + 128] = src[s, r * 9 + c]
                return carry

            lax.fori_loop(0, STREAM // 9, body, 0)

    write_head(gat_b, core)
    copy_i.wait_recv()
    write_head(gat_a, 1 - core)

    for i in range(2, CHUNKS):
        finish_text(i)

    send_ids_far.wait_send()
    send_ids_near.wait_send()
    for i in range(CHUNKS):
        forward(i).wait_send()
        near_part(i).wait_send()
        back(i).wait_send()
    for copy in [send_zt, copy_a, loss_a, copy_i] + copies_b + loss_b + copies_c + loss_c + copies_d + loss_d + copies_e + copies_g + copies_h:
        copy.wait_send()


def shards(image_emb, text_feat, text_head, pair_ids, row_weight):
    anywhere = pl.BlockSpec(memory_space=pl.ANY)
    vmem = pl.BlockSpec(memory_space=pltpu.VMEM)
    block = (ROWS, WIDTH)
    dma = pltpu.SemaphoreType.DMA
    unit = (16, 128)
    scratch = [
        pltpu.VMEM(block, BF16),
        pltpu.VMEM(block, BF16),
        pltpu.VMEM((WIDTH, WIDTH), BF16),
        pltpu.VMEM(block, BF16),
        pltpu.VMEM((ROWS, 1), F32),
        pltpu.VMEM(block, F32),
        pltpu.VMEM((ROWS, 1), F32),
        pltpu.VMEM(block, BF16),
        pltpu.VMEM(block, BF16),
        pltpu.VMEM(block, BF16),
        pltpu.VMEM(block, BF16),
        pltpu.VMEM((4, 128), jnp.int32),
        pltpu.VMEM((4, 128), jnp.int32),
        pltpu.VMEM(block, F32),
        pltpu.VMEM(block, F32),
        pltpu.VMEM(block, BF16),
        pltpu.VMEM(block, BF16),
        pltpu.VMEM(block, BF16),
        pltpu.VMEM(block, BF16),
        pltpu.VMEM(block, BF16),
        pltpu.VMEM(block, BF16),
        pltpu.VMEM((ROWS, ROWS), BF16),
        pltpu.VMEM((ROWS, ROWS), BF16),
        pltpu.VMEM((ROWS, ROWS), BF16),
        pltpu.VMEM((1, ROWS), F32),
        pltpu.VMEM((WIDTH, WIDTH), F32),
        pltpu.VMEM((UNITS,) + unit, BF16),
        pltpu.VMEM((HALF,) + unit, BF16),
        pltpu.VMEM((HALF + 16,) + unit, BF16),
        pltpu.VMEM((6, PIECE1) + unit, BF16),
        pltpu.VMEM((2, PIECE1) + unit, BF16),
        pltpu.VMEM((6, PIECE2) + unit, BF16),
        pltpu.VMEM((8 * PIECE3,) + unit, BF16),
        pltpu.VMEM((7, PIECE3) + unit, BF16),
        pltpu.VMEM((8 * PIECE3,) + unit, BF16),
        pltpu.VMEM((2, PIECE1) + unit, BF16),
        pltpu.VMEM((2, 4 * PIECE1) + unit, BF16),
        pltpu.VMEM((2, 4 * PIECE1) + unit, BF16),
        pltpu.VMEM((2, 8, 128), F32),
        pltpu.VMEM((4, 8, 128), F32),
        pltpu.VMEM((4, 8, 128), F32),
        pltpu.VMEM((8, 8, 128), F32),
        dma((3,)),
        dma((CHUNKS,)), dma((CHUNKS,)),
        dma((2,)), dma((2,)),
        dma, dma,
        dma((CHUNKS,)), dma((CHUNKS,)),
        dma((CHUNKS,)), dma((CHUNKS,)),
        dma, dma,
        dma((6,)), dma((6,)),
        dma((6,)), dma((6,)),
        dma((7,)), dma((7,)),
        dma((7,)), dma((7,)),
        dma((6,)), dma((6,)),
        dma((6,)), dma((6,)),
        dma, dma,
        dma((14,)), dma((14,)),
        pltpu.SemaphoreType.REGULAR,
    ]
    return pl.pallas_call(
        kernel,
        out_shape=(
            jax.ShapeDtypeStruct((1,), F32),
            jax.ShapeDtypeStruct(block, BF16),
            jax.ShapeDtypeStruct(block, BF16),
            jax.ShapeDtypeStruct((WIDTH, WIDTH), BF16),
        ),
        in_specs=[anywhere, anywhere, anywhere, vmem, vmem],
        out_specs=(pl.BlockSpec(memory_space=pltpu.SMEM), vmem, vmem, vmem),
        scratch_shapes=scratch,
        compiler_params=pltpu.CompilerParams(
            collective_id=0, has_side_effects=True, vmem_limit_bytes=58 * 1024 * 1024
        ),
        name="contrast",
    )(image_emb, text_feat, text_head, pair_ids.reshape(4, 128), row_weight.reshape(1, ROWS))


def solution(mesh):
    in_specs = (P("dp", None), P("dp", None), P(), P("dp"), P("dp"))
    out_specs = (P(), P("dp", None), P("dp", None), P())
    return jax.shard_map(shards, mesh=mesh, in_specs=in_specs, out_specs=out_specs, check_vma=False)
```

```python
import functools

import jax
import jax.numpy as jnp
from jax import lax
from jax.experimental import pallas as pl
from jax.experimental.pallas import tpu as pltpu
from jax.sharding import PartitionSpec as P

MESH = pl.DeviceIdType.MESH
F32 = jnp.float32
BF16 = jnp.bfloat16

SCALE = 10.0
BIAS = -2.0
EPS = 1e-06

ROWS = 512
WIDTH = 1152
CHUNK = 128
CHUNKS = ROWS // CHUNK
BACK = 64
BACKS = ROWS // BACK
BACK_1 = 4
BACK_2 = 5
PIECES = 4

UNITS = (WIDTH // 16) * (WIDTH // 128)
HALF = UNITS // 2
STREAM = HALF // 2
PIECE1 = 44
PIECE2 = 11
PIECE3 = 3


def dot_nt(a, b):
    return lax.dot_general(a, b, (((1,), (1,)), ((), ())), preferred_element_type=F32)


def dot_nn(a, b):
    return lax.dot_general(a, b, (((1,), (0,)), ((), ())), preferred_element_type=F32)


def dot_tn(a, b):
    return lax.dot_general(a, b, (((0,), (0,)), ((), ())), preferred_element_type=F32)


def rows_of(i, size=CHUNK):
    return pl.ds(pl.multiple_of(i * size, size), size)


def kernel(
    image_ref, text_ref, head_ref, ids_ref, weight_ref,
    loss_ref, gi_ref, gt_ref, gh_ref,
    image, text, head, zi, zi_inv, zt32, zt_inv, zt, zt_near, zt_far, text_far,
    ids_near, ids_far, dzt, dzi, part_near, got_near, part_far, got_far, du, du_far,
    dlog_own, dlog_near, dlog_far, loss_row, head_acc,
    units, got_a, half_b, got_b, sum_b, got_c, sum_c, got_d, gat_d, gat_c, gat_b, gat_a,
    loss_core, loss_x, loss_y, loss_z, gi, gt, gh,
    load_sem, f_send, f_recv, id_send, id_recv, n_send, n_recv, np_send, np_recv, r_send, r_recv,
    a_send, a_recv, b_send, b_recv, c_send, c_recv, d_send, d_recv,
    e_send, e_recv, g_send, g_recv, h_send, h_recv, i_send, i_recv,
    l_send, l_recv, gate_sem, out_sem,
):
    me = lax.axis_index("dp")
    core = me % 2
    x = (me // 2) % 4
    y = (me // 8) % 4
    z = me // 32

    def at(zz, yy, xx, cc):
        return ((zz * 4 + yy) * 4 + xx) * 2 + cc

    near = at(z, y, x, 1 - core)
    far = at((z + 4) % 8, y, x, core)

    def x_peer(d):
        return at(z, y, (x + d) % 4, core)

    def y_peer(d):
        return at(z, (y + d) % 4, x, core)

    def z_peer(d):
        return at((z + d) % 8, y, x, core)

    def remote(src, dst, send, recv, device):
        return pltpu.make_async_remote_copy(
            src_ref=src, dst_ref=dst, send_sem=send, recv_sem=recv,
            device_id=(device,), device_id_type=MESH,
        )

    loads = [
        pltpu.make_async_copy(head_ref, head, load_sem.at[0]),
        pltpu.make_async_copy(text_ref, text, load_sem.at[1]),
        pltpu.make_async_copy(image_ref, image, load_sem.at[2]),
    ]
    for load in loads:
        load.start()

    barrier = pltpu.get_barrier_semaphore()
    peers = [near] + [x_peer(d) for d in (1, 2, 3)] + [y_peer(d) for d in (1, 2, 3)] + [z_peer(d) for d in range(1, 8)]
    for peer in peers:
        pl.semaphore_signal(barrier, inc=1, device_id=(peer,), device_id_type=MESH)
    pl.semaphore_wait(barrier, len(peers))

    send_ids_far = remote(ids_ref, ids_far, id_send.at[0], id_recv.at[0], far)
    send_ids_near = remote(ids_ref, ids_near, id_send.at[1], id_recv.at[1], near)
    send_ids_far.start()
    send_ids_near.start()

    def forward(i):
        return remote(text_ref.at[rows_of(i)], text_far.at[rows_of(i)], f_send.at[i], f_recv.at[i], far)

    for i in range(CHUNKS):
        forward(i).start()

    loads[0].wait()
    loads[1].wait()

    def project(i, carry):
        rows = rows_of(i)
        u = dot_nn(text[rows, :], head[...])
        inv = 1.0 / jnp.sqrt(jnp.sum(u * u, axis=1, keepdims=True) + EPS)
        unit = u * inv
        zt32[rows, :] = unit
        zt_inv[rows, :] = inv
        zt[rows, :] = unit.astype(BF16)
        return carry

    lax.fori_loop(0, CHUNKS, project, 0)
    send_zt = remote(zt, zt_near, n_send, n_recv, near)
    send_zt.start()

    loads[2].wait()

    def image_norm(i, carry):
        rows = rows_of(i)
        v = image[rows, :].astype(F32)
        inv = 1.0 / jnp.sqrt(jnp.sum(v * v, axis=1, keepdims=True) + EPS)
        zi_inv[rows, :] = inv
        zi[rows, :] = (v * inv).astype(BF16)
        return carry

    lax.fori_loop(0, CHUNKS, image_norm, 0)

    own_ids = ids_ref[...]
    ids_image = jnp.concatenate([own_ids[i : i + 1, :] for i in range(CHUNKS)], axis=1)
    weight = weight_ref[...].astype(F32).reshape(1, ROWS)
    loss_row[...] = jnp.zeros_like(loss_row)

    def tile(texts, ids_row):
        s = dot_nt(texts, zi[...])
        logit = SCALE * s + BIAS
        ids_col = jnp.transpose(jnp.broadcast_to(ids_row, (CHUNK, CHUNK)))[:, :1]
        same = ids_col == ids_image
        v = jnp.where(same, -logit, logit)
        e = jnp.exp(-jnp.abs(v))
        soft = jnp.maximum(v, 0.0) + jnp.log1p(e)
        loss_row[...] += jnp.sum(soft, axis=0, keepdims=True)
        sig = jnp.where(v >= 0.0, 1.0, e) / (1.0 + e)
        d = (jnp.where(same, -weight, weight) * sig).astype(BF16)
        part = (SCALE * dot_nn(d, zi[...])).astype(BF16)
        return d, part

    def own_tile(i, carry):
        rows = rows_of(i)
        d, part = tile(zt[rows, :], ids_ref[pl.ds(i, 1), :])
        dlog_own[rows, :] = d
        dzt[rows, :] = part.astype(F32)
        return carry

    lax.fori_loop(0, CHUNKS, own_tile, 0)

    send_ids_near.wait_recv()
    send_zt.wait_recv()

    def near_part(i):
        return remote(part_near.at[rows_of(i)], got_near.at[rows_of(i)], np_send.at[i], np_recv.at[i], near)

    def near_tile(i, carry):
        rows = rows_of(i)
        d, part = tile(zt_near[rows, :], ids_near[pl.ds(i, 1), :])
        dlog_near[rows, :] = d
        part_near[rows, :] = part
        near_part(i).start()
        return carry

    lax.fori_loop(0, CHUNKS, near_tile, 0)

    def image_grad(i, carry):
        cols = rows_of(i)
        dzi[cols, :] = dot_tn(dlog_own[:, cols], zt[...]) + dot_tn(dlog_near[:, cols], zt_near[...])
        return carry

    lax.fori_loop(0, CHUNKS, image_grad, 0)

    def own_du(i, carry):
        rows = rows_of(i)
        near_part(i).wait_recv()
        g = dzt[rows, :] + got_near[rows, :].astype(F32)
        dzt[rows, :] = g
        unit = zt32[rows, :]
        du[rows, :] = ((g - unit * jnp.sum(unit * g, axis=1, keepdims=True)) * zt_inv[rows, :]).astype(BF16)
        return carry

    lax.fori_loop(0, CHUNKS, own_du, 0)

    def head_own(i, carry):
        cols = rows_of(i)
        head_acc[cols, :] = dot_tn(text[:, cols], du[...])
        return carry

    lax.fori_loop(0, WIDTH // 128, head_own, 0)

    send_ids_far.wait_recv()

    def back(i):
        rows = rows_of(i, BACK)
        return remote(part_far.at[rows], got_far.at[rows], r_send.at[i], r_recv.at[i], far)

    def send_back(first, last):
        for j in range(first, last):
            back(j).start()

    def far_tile(i):
        rows = rows_of(i)
        u = dot_nn(text_far[rows, :], head[...])
        inv = 1.0 / jnp.sqrt(jnp.sum(u * u, axis=1, keepdims=True) + EPS)
        unit = u * inv
        texts = unit.astype(BF16)
        zt_far[rows, :] = texts
        d, part = tile(texts, ids_far[pl.ds(i, 1), :])
        dlog_far[rows, :] = d
        part_far[rows, :] = part
        g = part.astype(F32)
        du_far[rows, :] = ((g - unit * jnp.sum(unit * g, axis=1, keepdims=True)) * inv).astype(BF16)

    def far_step(i, carry):
        forward(i).wait_recv()

        @pl.when(i == CHUNKS - 1)
        def _():
            pl.semaphore_signal(gate_sem, inc=1, device_id=(z_peer(6),), device_id_type=MESH)
            pl.semaphore_wait(gate_sem, 1)
            send_back(0, BACK_1)

        far_tile(i)
        return carry

    lax.fori_loop(0, CHUNKS, far_step, 0)

    def head_all(i, carry):
        i = (i + 4 * (1 - core)) % 9
        cols = rows_of(i)
        total = head_acc[cols, :] + dot_tn(text_far[:, cols], du_far[...])
        out = total.astype(BF16)
        for r in range(8):
            for c in range(9):
                units[i * 72 + (r * 9 + c)] = out[16 * r : 16 * r + 16, 128 * c : 128 * c + 128]
        return carry

    lax.fori_loop(0, 5, head_all, 0)
    copy_a = remote(units.at[pl.ds((1 - core) * HALF, HALF)], got_a, a_send, a_recv, near)
    copy_a.start()
    lax.fori_loop(5, 9, head_all, 0)
    loss_core[core] = jnp.broadcast_to(jnp.sum(weight * loss_row[...]).reshape(1, 1), (8, 128))

    loss_a = remote(loss_core.at[core], loss_core.at[core], l_send.at[0], l_recv.at[0], near)
    loss_a.start()

    def finish_image(i, carry):
        rows = rows_of(i)
        g = SCALE * (dzi[rows, :] + dot_tn(dlog_far[:, rows], zt_far[...]))
        inv = zi_inv[rows, :]
        unit = image[rows, :].astype(F32) * inv
        gi[rows, :] = ((g - unit * jnp.sum(unit * g, axis=1, keepdims=True)) * inv).astype(BF16)
        return carry

    def put_text(i):
        return pltpu.make_async_copy(gt.at[rows_of(i)], gt_ref.at[rows_of(i)], out_sem.at[i])

    def finish_text(i):
        for j in range(i * CHUNK // BACK, (i + 1) * CHUNK // BACK):
            back(j).wait_recv()
        rows = rows_of(i)
        g = dzt[rows, :] + got_far[rows, :].astype(F32)
        unit = zt32[rows, :]
        d = ((g - unit * jnp.sum(unit * g, axis=1, keepdims=True)) * zt_inv[rows, :]).astype(BF16)
        gt[rows, :] = dot_nt(d, head[...]).astype(BF16)
        put_text(i).start()

    copy_a.wait_recv()
    loss_a.wait_recv()
    loss_x[x] = loss_core[0] + loss_core[1]

    def add_a(i, carry):
        own = units[pl.ds(core * HALF + i * 12, 12)].astype(F32)
        half_b[pl.ds(i * 12, 12)] = (own + got_a[pl.ds(i * 12, 12)].astype(F32)).astype(BF16)
        return carry

    lax.fori_loop(0, HALF // 12, add_a, 0)
    half_b[pl.ds(HALF, 16)] = jnp.zeros((16, 16, 128), BF16)

    first = [(x_peer, x), (y_peer, y)]
    second = [(y_peer, y), (x_peer, x)]
    copies_b = []
    for s in range(2):
        peer, at_s = first[s]
        for d in (1, 2, 3):
            to = (at_s + d) % 4
            k = 3 * s + d - 1
            copies_b.append(remote(half_b.at[pl.ds(STREAM * s + PIECE1 * to, PIECE1)], got_b.at[k], b_send.at[k], b_recv.at[k], peer(d)))
    loss_b = [remote(loss_x.at[x], loss_x.at[x], l_send.at[d], l_recv.at[d], x_peer(d)) for d in (1, 2, 3)]
    for copy in copies_b + loss_b:
        copy.start()

    lax.fori_loop(0, CHUNKS, finish_image, 0)
    put_image = pltpu.make_async_copy(gi, gi_ref, out_sem.at[CHUNKS])
    put_image.start()

    for copy in copies_b + loss_b:
        copy.wait_recv()
    loss_y[y] = (loss_x[0] + loss_x[1]) + (loss_x[2] + loss_x[3])
    for s in range(2):
        base = STREAM * s + PIECE1 * first[s][1]

        def add_b(i, carry, s=s, base=base):
            total = half_b[pl.ds(base + i * 11, 11)].astype(F32)
            for k in range(3 * s, 3 * s + 3):
                total = total + got_b[k, pl.ds(i * 11, 11)].astype(F32)
            sum_b[s, pl.ds(i * 11, 11)] = total.astype(BF16)
            return carry

        lax.fori_loop(0, 4, add_b, 0)

    copies_c = []
    for s in range(2):
        peer, at_s = second[s]
        for d in (1, 2, 3):
            to = (at_s + d) % 4
            k = 3 * s + d - 1
            copies_c.append(remote(sum_b.at[s, pl.ds(PIECE2 * to, PIECE2)], got_c.at[k], c_send.at[k], c_recv.at[k], peer(d)))
    loss_c = [remote(loss_y.at[y], loss_y.at[y], l_send.at[3 + d], l_recv.at[3 + d], y_peer(d)) for d in (1, 2, 3)]
    for copy in copies_c + loss_c:
        copy.start()
    for copy in copies_c + loss_c:
        copy.wait_recv()
    loss_z[z] = (loss_y[0] + loss_y[1]) + (loss_y[2] + loss_y[3])
    for s in range(2):
        total = sum_b[s, pl.ds(PIECE2 * second[s][1], PIECE2)].astype(F32)
        for k in range(3 * s, 3 * s + 3):
            total = total + got_c[k].astype(F32)
        sum_c[pl.ds(PIECE2 * s, PIECE2)] = total.astype(BF16)
    sum_c[pl.ds(2 * PIECE2, 2)] = jnp.zeros((2, 16, 128), BF16)

    copies_d = []
    for d in range(1, 8):
        to = (z + d) % 8
        copies_d.append(remote(sum_c.at[pl.ds(PIECE3 * to, PIECE3)], got_d.at[d - 1], d_send.at[d - 1], d_recv.at[d - 1], z_peer(d)))
    loss_d = [remote(loss_z.at[z], loss_z.at[z], l_send.at[6 + d], l_recv.at[6 + d], z_peer(d)) for d in range(1, 8)]
    for copy in copies_d + loss_d:
        copy.start()
    send_back(BACK_1, BACK_2)
    for copy in copies_d + loss_d:
        copy.wait_recv()
    total = sum_c[pl.ds(PIECE3 * z, PIECE3)].astype(F32)
    for k in range(7):
        total = total + got_d[k].astype(F32)
    gat_d[pl.ds(PIECE3 * z, PIECE3)] = total.astype(BF16)
    sums = [loss_z[k] for k in range(8)]
    loss_all = ((sums[0] + sums[1]) + (sums[2] + sums[3])) + ((sums[4] + sums[5]) + (sums[6] + sums[7]))
    loss_ref[0] = jnp.max(loss_all) / (3.0 * ROWS * ROWS * 256)

    mine = gat_d.at[pl.ds(PIECE3 * z, PIECE3)]
    copies_e = [remote(mine, mine, e_send.at[d - 1], e_recv.at[d - 1], z_peer(d)) for d in range(1, 8)]
    for copy in copies_e:
        copy.start()
    finish_text(0)
    finish_text(1)
    for copy in copies_e:
        copy.wait_recv()
    send_back(BACK_2, BACKS)

    copies_g = []
    for s in range(2):
        peer, at_s = second[s]
        src = gat_d.at[pl.ds(PIECE2 * s, PIECE2)]
        dst = gat_c.at[s, pl.ds(PIECE2 * at_s, PIECE2)]
        for d in (1, 2, 3):
            k = 3 * s + d - 1
            copies_g.append(remote(src, dst, g_send.at[k], g_recv.at[k], peer(d)))
    for copy in copies_g:
        copy.start()
    for s in range(2):
        gat_c[s, pl.ds(PIECE2 * second[s][1], PIECE2)] = gat_d[pl.ds(PIECE2 * s, PIECE2)]
    for copy in copies_g:
        copy.wait_recv()

    copies_h = []
    for s in range(2):
        peer, at_s = first[s]
        dst = gat_b.at[s, pl.ds(PIECE1 * at_s, PIECE1)]
        for d in (1, 2, 3):
            k = 3 * s + d - 1
            copies_h.append(remote(gat_c.at[s], dst, h_send.at[k], h_recv.at[k], peer(d)))
    for copy in copies_h:
        copy.start()
    for s in range(2):
        gat_b[s, pl.ds(PIECE1 * first[s][1], PIECE1)] = gat_c[s]
    for copy in copies_h:
        copy.wait_recv()

    copy_i = remote(gat_b, gat_a, i_send, i_recv, near)
    copy_i.start()

    def write_head(src, which):
        for s in range(2):

            def body(r, carry, s=s):
                row = pl.ds(pl.multiple_of(which * (HALF // 9 * 16) + s * (STREAM // 9 * 16) + r * 16, 16), 16)
                for c in range(9):
                    gh[row, 128 * c : 128 * c + 128] = src[s, r * 9 + c]
                return carry

            lax.fori_loop(0, STREAM // 9, body, 0)

    def put_head(which, k):
        rows = rows_of(which, WIDTH // 2)
        return pltpu.make_async_copy(gh.at[rows], gh_ref.at[rows], out_sem.at[CHUNKS + 1 + k])

    write_head(gat_b, core)
    put_head(core, 0).start()
    copy_i.wait_recv()
    write_head(gat_a, 1 - core)
    put_head(1 - core, 1).start()

    for i in range(2, CHUNKS):
        finish_text(i)

    send_ids_far.wait_send()
    send_ids_near.wait_send()
    for i in range(CHUNKS):
        forward(i).wait_send()
        near_part(i).wait_send()
    for i in range(BACKS):
        back(i).wait_send()
    for copy in [send_zt, copy_a, loss_a, copy_i] + copies_b + loss_b + copies_c + loss_c + copies_d + loss_d + copies_e + copies_g + copies_h:
        copy.wait_send()
    for i in range(CHUNKS):
        put_text(i).wait()
    put_image.wait()
    put_head(core, 0).wait()
    put_head(1 - core, 1).wait()


def move(a_ref, b_ref, c_ref, a_out, b_out, c_out, a_buf, b_buf, c_buf, sem, sem2):
    ins = []
    outs = []
    for k, (src, buf, dst) in enumerate([(a_ref, a_buf, a_out), (b_ref, b_buf, b_out), (c_ref, c_buf, c_out)]):
        size = src.shape[0] // PIECES
        for i in range(PIECES):
            rows = pl.ds(i * size, size)
            ins.append(pltpu.make_async_copy(src.at[rows], buf.at[rows], sem.at[k * PIECES + i]))
            outs.append(pltpu.make_async_copy(buf.at[rows], dst.at[rows], sem2.at[k * PIECES + i]))
    for copy in ins:
        copy.start()
    for copy, out in zip(ins, outs):
        copy.wait()
        out.start()
    for copy in outs:
        copy.wait()


def shards(image_emb, text_feat, text_head, pair_ids, row_weight):
    anywhere = pl.BlockSpec(memory_space=pl.ANY)
    vmem = pl.BlockSpec(memory_space=pltpu.VMEM)
    block = (ROWS, WIDTH)
    dma = pltpu.SemaphoreType.DMA
    unit = (16, 128)
    scratch = [
        pltpu.VMEM(block, BF16),
        pltpu.VMEM(block, BF16),
        pltpu.VMEM((WIDTH, WIDTH), BF16),
        pltpu.VMEM(block, BF16),
        pltpu.VMEM((ROWS, 1), F32),
        pltpu.VMEM(block, F32),
        pltpu.VMEM((ROWS, 1), F32),
        pltpu.VMEM(block, BF16),
        pltpu.VMEM(block, BF16),
        pltpu.VMEM(block, BF16),
        pltpu.VMEM(block, BF16),
        pltpu.VMEM((4, 128), jnp.int32),
        pltpu.VMEM((4, 128), jnp.int32),
        pltpu.VMEM(block, F32),
        pltpu.VMEM(block, F32),
        pltpu.VMEM(block, BF16),
        pltpu.VMEM(block, BF16),
        pltpu.VMEM(block, BF16),
        pltpu.VMEM(block, BF16),
        pltpu.VMEM(block, BF16),
        pltpu.VMEM(block, BF16),
        pltpu.VMEM((ROWS, ROWS), BF16),
        pltpu.VMEM((ROWS, ROWS), BF16),
        pltpu.VMEM((ROWS, ROWS), BF16),
        pltpu.VMEM((1, ROWS), F32),
        pltpu.VMEM((WIDTH, WIDTH), F32),
        pltpu.VMEM((UNITS,) + unit, BF16),
        pltpu.VMEM((HALF,) + unit, BF16),
        pltpu.VMEM((HALF + 16,) + unit, BF16),
        pltpu.VMEM((6, PIECE1) + unit, BF16),
        pltpu.VMEM((2, PIECE1) + unit, BF16),
        pltpu.VMEM((6, PIECE2) + unit, BF16),
        pltpu.VMEM((8 * PIECE3,) + unit, BF16),
        pltpu.VMEM((7, PIECE3) + unit, BF16),
        pltpu.VMEM((8 * PIECE3,) + unit, BF16),
        pltpu.VMEM((2, PIECE1) + unit, BF16),
        pltpu.VMEM((2, 4 * PIECE1) + unit, BF16),
        pltpu.VMEM((2, 4 * PIECE1) + unit, BF16),
        pltpu.VMEM((2, 8, 128), F32),
        pltpu.VMEM((4, 8, 128), F32),
        pltpu.VMEM((4, 8, 128), F32),
        pltpu.VMEM((8, 8, 128), F32),
        pltpu.VMEM(block, BF16),
        pltpu.VMEM(block, BF16),
        pltpu.VMEM((WIDTH, WIDTH), BF16),
        dma((3,)),
        dma((CHUNKS,)), dma((CHUNKS,)),
        dma((2,)), dma((2,)),
        dma, dma,
        dma((CHUNKS,)), dma((CHUNKS,)),
        dma((BACKS,)), dma((BACKS,)),
        dma, dma,
        dma((6,)), dma((6,)),
        dma((6,)), dma((6,)),
        dma((7,)), dma((7,)),
        dma((7,)), dma((7,)),
        dma((6,)), dma((6,)),
        dma((6,)), dma((6,)),
        dma, dma,
        dma((14,)), dma((14,)),
        pltpu.SemaphoreType.REGULAR,
        dma((CHUNKS + 3,)),
    ]
    loss, *grads = pl.pallas_call(
        kernel,
        out_shape=(
            jax.ShapeDtypeStruct((1,), F32),
            jax.ShapeDtypeStruct(block, BF16),
            jax.ShapeDtypeStruct(block, BF16),
            jax.ShapeDtypeStruct((WIDTH, WIDTH), BF16),
        ),
        in_specs=[anywhere, anywhere, anywhere, vmem, vmem],
        out_specs=(pl.BlockSpec(memory_space=pltpu.SMEM), anywhere, anywhere, anywhere),
        scratch_shapes=scratch,
        compiler_params=pltpu.CompilerParams(
            collective_id=0, has_side_effects=True, vmem_limit_bytes=58 * 1024 * 1024
        ),
        name="contrast",
    )(image_emb, text_feat, text_head, pair_ids.reshape(4, 128), row_weight)
    moved = pl.pallas_call(
        move,
        out_shape=tuple(jax.ShapeDtypeStruct(g.shape, BF16) for g in grads),
        in_specs=[anywhere] * 3,
        out_specs=(anywhere,) * 3,
        scratch_shapes=[pltpu.VMEM(g.shape, BF16) for g in grads] + [dma((3 * PIECES,)), dma((3 * PIECES,))],
        name="move",
    )(*grads)
    return (loss, *moved)


def solution(mesh):
    in_specs = (P("dp", None), P("dp", None), P(), P("dp"), P("dp"))
    out_specs = (P(), P("dp", None), P("dp", None), P())
    return jax.shard_map(shards, mesh=mesh, in_specs=in_specs, out_specs=out_specs, check_vma=False)
```

```python
import functools

import jax
import jax.numpy as jnp
from jax import lax
from jax.experimental import pallas as pl
from jax.experimental.pallas import tpu as pltpu
from jax.sharding import PartitionSpec as P

MESH = pl.DeviceIdType.MESH
F32 = jnp.float32
BF16 = jnp.bfloat16

SCALE = 10.0
BIAS = -2.0
EPS = 1e-06

ROWS = 512
WIDTH = 1152
CHUNK = 128
CHUNKS = ROWS // CHUNK
BACK = 64
BACKS = ROWS // BACK
BACK_1 = 4
BACK_2 = 5

UNITS = (WIDTH // 16) * (WIDTH // 128)
HALF = UNITS // 2
STREAM = HALF // 2
PIECE1 = 44
PIECE2 = 11
PIECE3 = 3


def dot_nt(a, b):
    return lax.dot_general(a, b, (((1,), (1,)), ((), ())), preferred_element_type=F32)


def dot_nn(a, b):
    return lax.dot_general(a, b, (((1,), (0,)), ((), ())), preferred_element_type=F32)


def dot_tn(a, b):
    return lax.dot_general(a, b, (((0,), (0,)), ((), ())), preferred_element_type=F32)


def rows_of(i, size=CHUNK):
    return pl.ds(pl.multiple_of(i * size, size), size)


def kernel(
    image_ref, text_ref, head_ref, ids_ref, weight_ref,
    loss_ref, gi, gt, gh,
    image, text, head, zi, zi_inv, zt32, zt_inv, zt, zt_near, zt_far, text_far,
    ids_near, ids_far, dzt, dzi, part_near, got_near, part_far, got_far, du, du_far,
    dlog_own, dlog_near, dlog_far, loss_row, head_acc,
    units, got_a, half_b, got_b, sum_b, got_c, sum_c, got_d, gat_d, gat_c, gat_b, gat_a,
    loss_core, loss_x, loss_y, loss_z,
    load_sem, f_send, f_recv, id_send, id_recv, n_send, n_recv, np_send, np_recv, r_send, r_recv,
    a_send, a_recv, b_send, b_recv, c_send, c_recv, d_send, d_recv,
    e_send, e_recv, g_send, g_recv, h_send, h_recv, i_send, i_recv,
    l_send, l_recv, gate_sem,
):
    me = lax.axis_index("dp")
    core = me % 2
    x = (me // 2) % 4
    y = (me // 8) % 4
    z = me // 32

    def at(zz, yy, xx, cc):
        return ((zz * 4 + yy) * 4 + xx) * 2 + cc

    near = at(z, y, x, 1 - core)
    far = at((z + 4) % 8, y, x, core)

    def x_peer(d):
        return at(z, y, (x + d) % 4, core)

    def y_peer(d):
        return at(z, (y + d) % 4, x, core)

    def z_peer(d):
        return at((z + d) % 8, y, x, core)

    def remote(src, dst, send, recv, device):
        return pltpu.make_async_remote_copy(
            src_ref=src, dst_ref=dst, send_sem=send, recv_sem=recv,
            device_id=(device,), device_id_type=MESH,
        )

    loads = [
        pltpu.make_async_copy(head_ref, head, load_sem.at[0]),
        pltpu.make_async_copy(text_ref, text, load_sem.at[1]),
        pltpu.make_async_copy(image_ref, image, load_sem.at[2]),
    ]
    for load in loads:
        load.start()

    barrier = pltpu.get_barrier_semaphore()
    peers = [near] + [x_peer(d) for d in (1, 2, 3)] + [y_peer(d) for d in (1, 2, 3)] + [z_peer(d) for d in range(1, 8)]
    for peer in peers:
        pl.semaphore_signal(barrier, inc=1, device_id=(peer,), device_id_type=MESH)
    pl.semaphore_wait(barrier, len(peers))

    send_ids_far = remote(ids_ref, ids_far, id_send.at[0], id_recv.at[0], far)
    send_ids_near = remote(ids_ref, ids_near, id_send.at[1], id_recv.at[1], near)
    send_ids_far.start()
    send_ids_near.start()

    def forward(i):
        return remote(text_ref.at[rows_of(i)], text_far.at[rows_of(i)], f_send.at[i], f_recv.at[i], far)

    for i in range(CHUNKS):
        forward(i).start()

    loads[0].wait()
    loads[1].wait()

    def project(i, carry):
        rows = rows_of(i)
        u = dot_nn(text[rows, :], head[...])
        inv = 1.0 / jnp.sqrt(jnp.sum(u * u, axis=1, keepdims=True) + EPS)
        unit = u * inv
        zt32[rows, :] = unit
        zt_inv[rows, :] = inv
        zt[rows, :] = unit.astype(BF16)
        return carry

    lax.fori_loop(0, CHUNKS, project, 0)
    send_zt = remote(zt, zt_near, n_send, n_recv, near)
    send_zt.start()

    loads[2].wait()

    def image_norm(i, carry):
        rows = rows_of(i)
        v = image[rows, :].astype(F32)
        inv = 1.0 / jnp.sqrt(jnp.sum(v * v, axis=1, keepdims=True) + EPS)
        zi_inv[rows, :] = inv
        zi[rows, :] = (v * inv).astype(BF16)
        return carry

    lax.fori_loop(0, CHUNKS, image_norm, 0)

    own_ids = ids_ref[...]
    ids_image = jnp.concatenate([own_ids[i : i + 1, :] for i in range(CHUNKS)], axis=1)
    weight = weight_ref[...].astype(F32).reshape(1, ROWS)
    loss_row[...] = jnp.zeros_like(loss_row)

    def tile(texts, ids_row):
        s = dot_nt(texts, zi[...])
        logit = SCALE * s + BIAS
        ids_col = jnp.transpose(jnp.broadcast_to(ids_row, (CHUNK, CHUNK)))[:, :1]
        same = ids_col == ids_image
        v = jnp.where(same, -logit, logit)
        e = jnp.exp(-jnp.abs(v))
        soft = jnp.maximum(v, 0.0) + jnp.log1p(e)
        loss_row[...] += jnp.sum(soft, axis=0, keepdims=True)
        sig = jnp.where(v >= 0.0, 1.0, e) / (1.0 + e)
        d = (jnp.where(same, -weight, weight) * sig).astype(BF16)
        part = (SCALE * dot_nn(d, zi[...])).astype(BF16)
        return d, part

    def own_tile(i, carry):
        rows = rows_of(i)
        d, part = tile(zt[rows, :], ids_ref[pl.ds(i, 1), :])
        dlog_own[rows, :] = d
        dzt[rows, :] = part.astype(F32)
        return carry

    lax.fori_loop(0, CHUNKS, own_tile, 0)

    send_ids_near.wait_recv()
    send_zt.wait_recv()

    def near_part(i):
        return remote(part_near.at[rows_of(i)], got_near.at[rows_of(i)], np_send.at[i], np_recv.at[i], near)

    def near_tile(i, carry):
        rows = rows_of(i)
        d, part = tile(zt_near[rows, :], ids_near[pl.ds(i, 1), :])
        dlog_near[rows, :] = d
        part_near[rows, :] = part
        near_part(i).start()
        return carry

    lax.fori_loop(0, CHUNKS, near_tile, 0)

    def image_grad(i, carry):
        cols = rows_of(i)
        dzi[cols, :] = dot_tn(dlog_own[:, cols], zt[...]) + dot_tn(dlog_near[:, cols], zt_near[...])
        return carry

    lax.fori_loop(0, CHUNKS, image_grad, 0)

    def own_du(i, carry):
        rows = rows_of(i)
        near_part(i).wait_recv()
        g = dzt[rows, :] + got_near[rows, :].astype(F32)
        dzt[rows, :] = g
        unit = zt32[rows, :]
        du[rows, :] = ((g - unit * jnp.sum(unit * g, axis=1, keepdims=True)) * zt_inv[rows, :]).astype(BF16)
        return carry

    lax.fori_loop(0, CHUNKS, own_du, 0)

    def head_own(i, carry):
        cols = rows_of(i)
        head_acc[cols, :] = dot_tn(text[:, cols], du[...])
        return carry

    lax.fori_loop(0, WIDTH // 128, head_own, 0)

    send_ids_far.wait_recv()

    def back(i):
        rows = rows_of(i, BACK)
        return remote(part_far.at[rows], got_far.at[rows], r_send.at[i], r_recv.at[i], far)

    def send_back(first, last):
        for j in range(first, last):
            back(j).start()

    def far_tile(i):
        rows = rows_of(i)
        u = dot_nn(text_far[rows, :], head[...])
        inv = 1.0 / jnp.sqrt(jnp.sum(u * u, axis=1, keepdims=True) + EPS)
        unit = u * inv
        texts = unit.astype(BF16)
        zt_far[rows, :] = texts
        d, part = tile(texts, ids_far[pl.ds(i, 1), :])
        dlog_far[rows, :] = d
        part_far[rows, :] = part
        g = part.astype(F32)
        du_far[rows, :] = ((g - unit * jnp.sum(unit * g, axis=1, keepdims=True)) * inv).astype(BF16)

    early = pl.ds(0, ROWS - CHUNK)
    late = pl.ds(ROWS - CHUNK, CHUNK)

    def head_early(i, carry):
        cols = rows_of(i)
        head_acc[cols, :] += dot_tn(text_far[early, cols], du_far[early, :])
        return carry

    def far_step(i, carry):
        forward(i).wait_recv()

        @pl.when(i == CHUNKS - 1)
        def _():
            pl.semaphore_signal(gate_sem, inc=1, device_id=(z_peer(6),), device_id_type=MESH)
            pl.semaphore_wait(gate_sem, 1)
            send_back(0, BACK_1)

        far_tile(i)

        @pl.when(i == CHUNKS - 2)
        def _():
            lax.fori_loop(0, WIDTH // 128, head_early, 0)

        return carry

    lax.fori_loop(0, CHUNKS, far_step, 0)

    def head_all(i, carry):
        i = (i + 4 * (1 - core)) % 9
        cols = rows_of(i)
        total = head_acc[cols, :] + dot_tn(text_far[late, cols], du_far[late, :])
        out = total.astype(BF16)
        for r in range(8):
            for c in range(9):
                units[i * 72 + (r * 9 + c)] = out[16 * r : 16 * r + 16, 128 * c : 128 * c + 128]
        return carry

    lax.fori_loop(0, 5, head_all, 0)
    copy_a = remote(units.at[pl.ds((1 - core) * HALF, HALF)], got_a, a_send, a_recv, near)
    copy_a.start()
    lax.fori_loop(5, 9, head_all, 0)
    loss_core[core] = jnp.broadcast_to(jnp.sum(weight * loss_row[...]).reshape(1, 1), (8, 128))

    loss_a = remote(loss_core.at[core], loss_core.at[core], l_send.at[0], l_recv.at[0], near)
    loss_a.start()

    def finish_image(i, carry):
        rows = rows_of(i)
        g = SCALE * (dzi[rows, :] + dot_tn(dlog_far[:, rows], zt_far[...]))
        inv = zi_inv[rows, :]
        unit = image[rows, :].astype(F32) * inv
        gi[rows, :] = ((g - unit * jnp.sum(unit * g, axis=1, keepdims=True)) * inv).astype(BF16)
        return carry

    def finish_text(i):
        for j in range(i * CHUNK // BACK, (i + 1) * CHUNK // BACK):
            back(j).wait_recv()
        rows = rows_of(i)
        g = dzt[rows, :] + got_far[rows, :].astype(F32)
        unit = zt32[rows, :]
        d = ((g - unit * jnp.sum(unit * g, axis=1, keepdims=True)) * zt_inv[rows, :]).astype(BF16)
        gt[rows, :] = dot_nt(d, head[...]).astype(BF16)

    copy_a.wait_recv()
    loss_a.wait_recv()
    loss_x[x] = loss_core[0] + loss_core[1]

    def add_a(i, carry):
        own = units[pl.ds(core * HALF + i * 12, 12)].astype(F32)
        half_b[pl.ds(i * 12, 12)] = (own + got_a[pl.ds(i * 12, 12)].astype(F32)).astype(BF16)
        return carry

    lax.fori_loop(0, HALF // 12, add_a, 0)
    half_b[pl.ds(HALF, 16)] = jnp.zeros((16, 16, 128), BF16)

    first = [(x_peer, x), (y_peer, y)]
    second = [(y_peer, y), (x_peer, x)]
    copies_b = []
    for e in (1, 2, 3, 0):
        for s in range(2):
            peer, at_s = first[s]
            part = (second[s][1] + e) % 4
            for d in (1, 2, 3):
                to = (at_s + d) % 4
                k = 3 * s + d - 1
                src = half_b.at[pl.ds(STREAM * s + PIECE1 * to + PIECE2 * part, PIECE2)]
                copies_b.append(remote(src, got_b.at[e, k], b_send.at[e, k], b_recv.at[e, k], peer(d)))
    loss_b = [remote(loss_x.at[x], loss_x.at[x], l_send.at[d], l_recv.at[d], x_peer(d)) for d in (1, 2, 3)]
    for copy in copies_b + loss_b:
        copy.start()

    lax.fori_loop(0, CHUNKS, finish_image, 0)

    copies_c = []
    for n, e in enumerate((1, 2, 3, 0)):
        for copy in copies_b[6 * n : 6 * n + 6]:
            copy.wait_recv()
        for s in range(2):
            peer, at_s = second[s]
            part = (at_s + e) % 4
            total = half_b[pl.ds(STREAM * s + PIECE1 * first[s][1] + PIECE2 * part, PIECE2)].astype(F32)
            for k in range(3 * s, 3 * s + 3):
                total = total + got_b[e, k].astype(F32)
            sum_b[s, pl.ds(PIECE2 * part, PIECE2)] = total.astype(BF16)
            if e > 0:
                k = 3 * s + e - 1
                copy = remote(sum_b.at[s, pl.ds(PIECE2 * part, PIECE2)], got_c.at[k], c_send.at[k], c_recv.at[k], peer(e))
                copy.start()
                copies_c.append(copy)
    for copy in loss_b:
        copy.wait_recv()
    loss_y[y] = (loss_x[0] + loss_x[1]) + (loss_x[2] + loss_x[3])
    loss_c = [remote(loss_y.at[y], loss_y.at[y], l_send.at[3 + d], l_recv.at[3 + d], y_peer(d)) for d in (1, 2, 3)]
    for copy in loss_c:
        copy.start()
    for copy in copies_c + loss_c:
        copy.wait_recv()
    loss_z[z] = (loss_y[0] + loss_y[1]) + (loss_y[2] + loss_y[3])
    for s in range(2):
        total = sum_b[s, pl.ds(PIECE2 * second[s][1], PIECE2)].astype(F32)
        for k in range(3 * s, 3 * s + 3):
            total = total + got_c[k].astype(F32)
        sum_c[pl.ds(PIECE2 * s, PIECE2)] = total.astype(BF16)
    sum_c[pl.ds(2 * PIECE2, 2)] = jnp.zeros((2, 16, 128), BF16)

    copies_d = []
    for d in range(1, 8):
        to = (z + d) % 8
        copies_d.append(remote(sum_c.at[pl.ds(PIECE3 * to, PIECE3)], got_d.at[d - 1], d_send.at[d - 1], d_recv.at[d - 1], z_peer(d)))
    loss_d = [remote(loss_z.at[z], loss_z.at[z], l_send.at[6 + d], l_recv.at[6 + d], z_peer(d)) for d in range(1, 8)]
    for copy in copies_d + loss_d:
        copy.start()
    send_back(BACK_1, BACK_2)
    for copy in copies_d + loss_d:
        copy.wait_recv()
    total = sum_c[pl.ds(PIECE3 * z, PIECE3)].astype(F32)
    for k in range(7):
        total = total + got_d[k].astype(F32)
    gat_d[pl.ds(PIECE3 * z, PIECE3)] = total.astype(BF16)
    sums = [loss_z[k] for k in range(8)]
    loss_all = ((sums[0] + sums[1]) + (sums[2] + sums[3])) + ((sums[4] + sums[5]) + (sums[6] + sums[7]))
    loss_ref[0] = jnp.max(loss_all) / (3.0 * ROWS * ROWS * 256)

    mine = gat_d.at[pl.ds(PIECE3 * z, PIECE3)]
    copies_e = [remote(mine, mine, e_send.at[d - 1], e_recv.at[d - 1], z_peer(d)) for d in range(1, 8)]
    for copy in copies_e:
        copy.start()
    finish_text(0)
    finish_text(1)
    for copy in copies_e:
        copy.wait_recv()
    send_back(BACK_2, BACKS)

    copies_g = []
    for s in range(2):
        peer, at_s = second[s]
        src = gat_d.at[pl.ds(PIECE2 * s, PIECE2)]
        dst = gat_c.at[s, pl.ds(PIECE2 * at_s, PIECE2)]
        for d in (1, 2, 3):
            k = 3 * s + d - 1
            copies_g.append(remote(src, dst, g_send.at[k], g_recv.at[k], peer(d)))
    for copy in copies_g:
        copy.start()
    for s in range(2):
        gat_c[s, pl.ds(PIECE2 * second[s][1], PIECE2)] = gat_d[pl.ds(PIECE2 * s, PIECE2)]
    for copy in copies_g:
        copy.wait_recv()

    copies_h = []
    for s in range(2):
        peer, at_s = first[s]
        dst = gat_b.at[s, pl.ds(PIECE1 * at_s, PIECE1)]
        for d in (1, 2, 3):
            k = 3 * s + d - 1
            copies_h.append(remote(gat_c.at[s], dst, h_send.at[k], h_recv.at[k], peer(d)))
    for copy in copies_h:
        copy.start()
    for s in range(2):
        gat_b[s, pl.ds(PIECE1 * first[s][1], PIECE1)] = gat_c[s]
    for copy in copies_h:
        copy.wait_recv()

    copy_i = remote(gat_b, gat_a, i_send, i_recv, near)
    copy_i.start()

    def write_head(src, which):
        for s in range(2):

            def body(r, carry, s=s):
                row = pl.ds(pl.multiple_of(which * (HALF // 9 * 16) + s * (STREAM // 9 * 16) + r * 16, 16), 16)
                for c in range(9):
                    gh[row, 128 * c : 128 * c + 128] = src[s, r * 9 + c]
                return carry

            lax.fori_loop(0, STREAM // 9, body, 0)

    write_head(gat_b, core)
    copy_i.wait_recv()
    write_head(gat_a, 1 - core)

    for i in range(2, CHUNKS):
        finish_text(i)

    send_ids_far.wait_send()
    send_ids_near.wait_send()
    for i in range(CHUNKS):
        forward(i).wait_send()
        near_part(i).wait_send()
    for i in range(BACKS):
        back(i).wait_send()
    for copy in [send_zt, copy_a, loss_a, copy_i] + copies_b + loss_b + copies_c + loss_c + copies_d + loss_d + copies_e + copies_g + copies_h:
        copy.wait_send()


def shards(image_emb, text_feat, text_head, pair_ids, row_weight):
    anywhere = pl.BlockSpec(memory_space=pl.ANY)
    vmem = pl.BlockSpec(memory_space=pltpu.VMEM)
    block = (ROWS, WIDTH)
    dma = pltpu.SemaphoreType.DMA
    unit = (16, 128)
    scratch = [
        pltpu.VMEM(block, BF16),
        pltpu.VMEM(block, BF16),
        pltpu.VMEM((WIDTH, WIDTH), BF16),
        pltpu.VMEM(block, BF16),
        pltpu.VMEM((ROWS, 1), F32),
        pltpu.VMEM(block, F32),
        pltpu.VMEM((ROWS, 1), F32),
        pltpu.VMEM(block, BF16),
        pltpu.VMEM(block, BF16),
        pltpu.VMEM(block, BF16),
        pltpu.VMEM(block, BF16),
        pltpu.VMEM((4, 128), jnp.int32),
        pltpu.VMEM((4, 128), jnp.int32),
        pltpu.VMEM(block, F32),
        pltpu.VMEM(block, F32),
        pltpu.VMEM(block, BF16),
        pltpu.VMEM(block, BF16),
        pltpu.VMEM(block, BF16),
        pltpu.VMEM(block, BF16),
        pltpu.VMEM(block, BF16),
        pltpu.VMEM(block, BF16),
        pltpu.VMEM((ROWS, ROWS), BF16),
        pltpu.VMEM((ROWS, ROWS), BF16),
        pltpu.VMEM((ROWS, ROWS), BF16),
        pltpu.VMEM((1, ROWS), F32),
        pltpu.VMEM((WIDTH, WIDTH), F32),
        pltpu.VMEM((UNITS,) + unit, BF16),
        pltpu.VMEM((HALF,) + unit, BF16),
        pltpu.VMEM((HALF + 16,) + unit, BF16),
        pltpu.VMEM((4, 6, PIECE2) + unit, BF16),
        pltpu.VMEM((2, PIECE1) + unit, BF16),
        pltpu.VMEM((6, PIECE2) + unit, BF16),
        pltpu.VMEM((8 * PIECE3,) + unit, BF16),
        pltpu.VMEM((7, PIECE3) + unit, BF16),
        pltpu.VMEM((8 * PIECE3,) + unit, BF16),
        pltpu.VMEM((2, PIECE1) + unit, BF16),
        pltpu.VMEM((2, 4 * PIECE1) + unit, BF16),
        pltpu.VMEM((2, 4 * PIECE1) + unit, BF16),
        pltpu.VMEM((2, 8, 128), F32),
        pltpu.VMEM((4, 8, 128), F32),
        pltpu.VMEM((4, 8, 128), F32),
        pltpu.VMEM((8, 8, 128), F32),
        dma((3,)),
        dma((CHUNKS,)), dma((CHUNKS,)),
        dma((2,)), dma((2,)),
        dma, dma,
        dma((CHUNKS,)), dma((CHUNKS,)),
        dma((BACKS,)), dma((BACKS,)),
        dma, dma,
        dma((4, 6)), dma((4, 6)),
        dma((6,)), dma((6,)),
        dma((7,)), dma((7,)),
        dma((7,)), dma((7,)),
        dma((6,)), dma((6,)),
        dma((6,)), dma((6,)),
        dma, dma,
        dma((14,)), dma((14,)),
        pltpu.SemaphoreType.REGULAR,
    ]
    outs = pl.pallas_call(
        kernel,
        out_shape=(
            jax.ShapeDtypeStruct((1,), F32),
            pltpu.VMEM(block, BF16),
            pltpu.VMEM(block, BF16),
            pltpu.VMEM((WIDTH, WIDTH), BF16),
        ),
        in_specs=[anywhere, anywhere, anywhere, vmem, vmem],
        out_specs=(pl.BlockSpec(memory_space=pltpu.SMEM), vmem, vmem, vmem),
        scratch_shapes=scratch,
        compiler_params=pltpu.CompilerParams(
            collective_id=0, has_side_effects=True, vmem_limit_bytes=50 * 1024 * 1024
        ),
        name="contrast",
    )(image_emb, text_feat, text_head, pair_ids.reshape(4, 128), row_weight)
    return tuple(outs)


def solution(mesh):
    in_specs = (P("dp", None), P("dp", None), P(), P("dp"), P("dp"))
    out_specs = (P(), P("dp", None), P("dp", None), P())
    return jax.shard_map(shards, mesh=mesh, in_specs=in_specs, out_specs=out_specs, check_vma=False)
```

```python
import functools

import jax
import jax.numpy as jnp
from jax import lax
from jax.experimental import pallas as pl
from jax.experimental.pallas import tpu as pltpu
from jax.sharding import PartitionSpec as P

MESH = pl.DeviceIdType.MESH
F32 = jnp.float32
BF16 = jnp.bfloat16

SCALE = 10.0
BIAS = -2.0
EPS = 1e-06

ROWS = 512
WIDTH = 1152
CHUNK = 128
CHUNKS = ROWS // CHUNK
BACK = 64
BACKS = ROWS // BACK
BACK_1 = 4
BACK_2 = 4

UNITS = (WIDTH // 16) * (WIDTH // 128)
HALF = UNITS // 2
STREAM = HALF // 2
PIECE1 = 44
PIECE2 = 11
PIECE3 = 3


def dot_nt(a, b):
    return lax.dot_general(a, b, (((1,), (1,)), ((), ())), preferred_element_type=F32)


def dot_nn(a, b):
    return lax.dot_general(a, b, (((1,), (0,)), ((), ())), preferred_element_type=F32)


def dot_tn(a, b):
    return lax.dot_general(a, b, (((0,), (0,)), ((), ())), preferred_element_type=F32)


def rows_of(i, size=CHUNK):
    return pl.ds(pl.multiple_of(i * size, size), size)


def kernel(
    image_ref, text_ref, head_ref, ids_ref, weight_ref,
    loss_ref, gi, gt, gh,
    image, text, head, zi, zi_inv, zt32, zt_inv, zt, zt_near, zt_far, text_far,
    ids_near, ids_far, dzt, dzi, part_near, got_near, part_far, got_far, du, du_far,
    dlog_own, dlog_near, dlog_far, loss_row, head_acc,
    units, got_a, half_b, got_b, sum_b, got_c, sum_c, got_d, gat_d, gat_c, gat_b, gat_a,
    loss_core, loss_x, loss_y, loss_z,
    load_sem, f_send, f_recv, id_send, id_recv, n_send, n_recv, np_send, np_recv, r_send, r_recv,
    a_send, a_recv, b_send, b_recv, c_send, c_recv, d_send, d_recv,
    e_send, e_recv, g_send, g_recv, h_send, h_recv, i_send, i_recv,
    l_send, l_recv, gate_sem,
):
    me = lax.axis_index("dp")
    core = me % 2
    x = (me // 2) % 4
    y = (me // 8) % 4
    z = me // 32

    def at(zz, yy, xx, cc):
        return ((zz * 4 + yy) * 4 + xx) * 2 + cc

    near = at(z, y, x, 1 - core)
    far = at((z + 4) % 8, y, x, core)

    def x_peer(d):
        return at(z, y, (x + d) % 4, core)

    def y_peer(d):
        return at(z, (y + d) % 4, x, core)

    def z_peer(d):
        return at((z + d) % 8, y, x, core)

    def remote(src, dst, send, recv, device):
        return pltpu.make_async_remote_copy(
            src_ref=src, dst_ref=dst, send_sem=send, recv_sem=recv,
            device_id=(device,), device_id_type=MESH,
        )

    loads = [
        pltpu.make_async_copy(head_ref, head, load_sem.at[0]),
        pltpu.make_async_copy(text_ref, text, load_sem.at[1]),
        pltpu.make_async_copy(image_ref, image, load_sem.at[2]),
    ]
    for load in loads:
        load.start()

    barrier = pltpu.get_barrier_semaphore()
    peers = [near] + [x_peer(d) for d in (1, 2, 3)] + [y_peer(d) for d in (1, 2, 3)] + [z_peer(d) for d in range(1, 8)]
    for peer in peers:
        pl.semaphore_signal(barrier, inc=1, device_id=(peer,), device_id_type=MESH)
    pl.semaphore_wait(barrier, len(peers))

    send_ids_far = remote(ids_ref, ids_far, id_send.at[0], id_recv.at[0], far)
    send_ids_near = remote(ids_ref, ids_near, id_send.at[1], id_recv.at[1], near)
    send_ids_far.start()
    send_ids_near.start()

    def forward(i):
        return remote(text_ref.at[rows_of(i)], text_far.at[rows_of(i)], f_send.at[i], f_recv.at[i], far)

    for i in range(CHUNKS):
        forward(i).start()

    loads[0].wait()
    loads[1].wait()

    def project(i, carry):
        rows = rows_of(i)
        u = dot_nn(text[rows, :], head[...])
        inv = 1.0 / jnp.sqrt(jnp.sum(u * u, axis=1, keepdims=True) + EPS)
        unit = u * inv
        zt32[rows, :] = unit
        zt_inv[rows, :] = inv
        zt[rows, :] = unit.astype(BF16)
        return carry

    lax.fori_loop(0, CHUNKS, project, 0)
    send_zt = remote(zt, zt_near, n_send, n_recv, near)
    send_zt.start()

    loads[2].wait()

    def image_norm(i, carry):
        rows = rows_of(i)
        v = image[rows, :].astype(F32)
        inv = 1.0 / jnp.sqrt(jnp.sum(v * v, axis=1, keepdims=True) + EPS)
        zi_inv[rows, :] = inv
        zi[rows, :] = (v * inv).astype(BF16)
        return carry

    lax.fori_loop(0, CHUNKS, image_norm, 0)

    own_ids = ids_ref[...]
    ids_image = jnp.concatenate([own_ids[i : i + 1, :] for i in range(CHUNKS)], axis=1)
    weight = weight_ref[...].astype(F32).reshape(1, ROWS)
    loss_row[...] = jnp.zeros_like(loss_row)

    def tile(texts, ids_row):
        s = dot_nt(texts, zi[...])
        logit = SCALE * s + BIAS
        ids_col = jnp.transpose(jnp.broadcast_to(ids_row, (CHUNK, CHUNK)))[:, :1]
        same = ids_col == ids_image
        v = jnp.where(same, -logit, logit)
        e = jnp.exp(-jnp.abs(v))
        soft = jnp.maximum(v, 0.0) + jnp.log1p(e)
        loss_row[...] += jnp.sum(soft, axis=0, keepdims=True)
        sig = jnp.where(v >= 0.0, 1.0, e) / (1.0 + e)
        d = (jnp.where(same, -weight, weight) * sig).astype(BF16)
        part = (SCALE * dot_nn(d, zi[...])).astype(BF16)
        return d, part

    def own_tile(i, carry):
        rows = rows_of(i)
        d, part = tile(zt[rows, :], ids_ref[pl.ds(i, 1), :])
        dlog_own[rows, :] = d
        dzt[rows, :] = part.astype(F32)
        return carry

    lax.fori_loop(0, CHUNKS, own_tile, 0)

    send_ids_near.wait_recv()
    send_zt.wait_recv()

    def near_part(i):
        return remote(part_near.at[rows_of(i)], got_near.at[rows_of(i)], np_send.at[i], np_recv.at[i], near)

    def near_tile(i, carry):
        rows = rows_of(i)
        d, part = tile(zt_near[rows, :], ids_near[pl.ds(i, 1), :])
        dlog_near[rows, :] = d
        part_near[rows, :] = part
        near_part(i).start()
        return carry

    lax.fori_loop(0, CHUNKS, near_tile, 0)

    def image_grad(i, carry):
        cols = rows_of(i)
        dzi[cols, :] = dot_tn(dlog_own[:, cols], zt[...]) + dot_tn(dlog_near[:, cols], zt_near[...])
        return carry

    lax.fori_loop(0, CHUNKS, image_grad, 0)

    def own_du(i, carry):
        rows = rows_of(i)
        near_part(i).wait_recv()
        g = dzt[rows, :] + got_near[rows, :].astype(F32)
        dzt[rows, :] = g
        unit = zt32[rows, :]
        du[rows, :] = ((g - unit * jnp.sum(unit * g, axis=1, keepdims=True)) * zt_inv[rows, :]).astype(BF16)
        return carry

    lax.fori_loop(0, CHUNKS, own_du, 0)

    def head_own(i, carry):
        cols = rows_of(i)
        head_acc[cols, :] = dot_tn(text[:, cols], du[...])
        return carry

    lax.fori_loop(0, WIDTH // 128, head_own, 0)

    send_ids_far.wait_recv()

    def back(i):
        rows = rows_of(i, BACK)
        return remote(part_far.at[rows], got_far.at[rows], r_send.at[i], r_recv.at[i], far)

    def send_back(first, last):
        for j in range(first, last):
            back(j).start()

    def far_tile(i):
        rows = rows_of(i)
        u = dot_nn(text_far[rows, :], head[...])
        inv = 1.0 / jnp.sqrt(jnp.sum(u * u, axis=1, keepdims=True) + EPS)
        unit = u * inv
        texts = unit.astype(BF16)
        zt_far[rows, :] = texts
        d, part = tile(texts, ids_far[pl.ds(i, 1), :])
        dlog_far[rows, :] = d
        part_far[rows, :] = part
        g = part.astype(F32)
        du_far[rows, :] = ((g - unit * jnp.sum(unit * g, axis=1, keepdims=True)) * inv).astype(BF16)

    early = pl.ds(0, ROWS - CHUNK)
    late = pl.ds(ROWS - CHUNK, CHUNK)

    def head_early(i, carry):
        cols = rows_of(i)
        head_acc[cols, :] += dot_tn(text_far[early, cols], du_far[early, :])
        return carry

    def far_step(i, carry):
        forward(i).wait_recv()

        @pl.when(i == CHUNKS - 1)
        def _():
            pl.semaphore_signal(gate_sem, inc=1, device_id=(z_peer(6),), device_id_type=MESH)
            pl.semaphore_wait(gate_sem, 1)
            send_back(0, BACK_1)

        far_tile(i)

        @pl.when(i == CHUNKS - 2)
        def _():
            lax.fori_loop(0, WIDTH // 128, head_early, 0)

        return carry

    lax.fori_loop(0, CHUNKS, far_step, 0)

    def head_all(i, carry):
        i = (i + 4 * (1 - core)) % 9
        cols = rows_of(i)
        total = head_acc[cols, :] + dot_tn(text_far[late, cols], du_far[late, :])
        out = total.astype(BF16)
        for r in range(8):
            for c in range(9):
                units[i * 72 + (r * 9 + c)] = out[16 * r : 16 * r + 16, 128 * c : 128 * c + 128]
        return carry

    lax.fori_loop(0, 5, head_all, 0)
    copy_a = remote(units.at[pl.ds((1 - core) * HALF, HALF)], got_a, a_send, a_recv, near)
    copy_a.start()
    lax.fori_loop(5, 9, head_all, 0)
    loss_core[core] = jnp.broadcast_to(jnp.sum(weight * loss_row[...]).reshape(1, 1), (8, 128))

    loss_a = remote(loss_core.at[core], loss_core.at[core], l_send.at[0], l_recv.at[0], near)
    loss_a.start()

    def finish_image(i, carry):
        rows = rows_of(i)
        g = SCALE * (dzi[rows, :] + dot_tn(dlog_far[:, rows], zt_far[...]))
        inv = zi_inv[rows, :]
        unit = image[rows, :].astype(F32) * inv
        gi[rows, :] = ((g - unit * jnp.sum(unit * g, axis=1, keepdims=True)) * inv).astype(BF16)
        return carry

    def finish_text(i):
        for j in range(i * CHUNK // BACK, (i + 1) * CHUNK // BACK):
            back(j).wait_recv()
        rows = rows_of(i)
        g = dzt[rows, :] + got_far[rows, :].astype(F32)
        unit = zt32[rows, :]
        d = ((g - unit * jnp.sum(unit * g, axis=1, keepdims=True)) * zt_inv[rows, :]).astype(BF16)
        gt[rows, :] = dot_nt(d, head[...]).astype(BF16)

    copy_a.wait_recv()
    loss_a.wait_recv()
    loss_x[x] = loss_core[0] + loss_core[1]

    def add_a(i, carry):
        own = units[pl.ds(core * HALF + i * 12, 12)].astype(F32)
        half_b[pl.ds(i * 12, 12)] = (own + got_a[pl.ds(i * 12, 12)].astype(F32)).astype(BF16)
        return carry

    lax.fori_loop(0, HALF // 12, add_a, 0)
    half_b[pl.ds(HALF, 16)] = jnp.zeros((16, 16, 128), BF16)

    first = [(x_peer, x), (y_peer, y)]
    second = [(y_peer, y), (x_peer, x)]
    copies_b = []
    for e in (1, 2, 3, 0):
        for s in range(2):
            peer, at_s = first[s]
            part = (second[s][1] + e) % 4
            for d in (1, 2, 3):
                to = (at_s + d) % 4
                k = 3 * s + d - 1
                src = half_b.at[pl.ds(STREAM * s + PIECE1 * to + PIECE2 * part, PIECE2)]
                copies_b.append(remote(src, got_b.at[e, k], b_send.at[e, k], b_recv.at[e, k], peer(d)))
    loss_b = [remote(loss_x.at[x], loss_x.at[x], l_send.at[d], l_recv.at[d], x_peer(d)) for d in (1, 2, 3)]
    for copy in copies_b + loss_b:
        copy.start()

    lax.fori_loop(0, CHUNKS, finish_image, 0)

    copies_c = []
    for n, e in enumerate((1, 2, 3, 0)):
        for copy in copies_b[6 * n : 6 * n + 6]:
            copy.wait_recv()
        for s in range(2):
            peer, at_s = second[s]
            part = (at_s + e) % 4
            total = half_b[pl.ds(STREAM * s + PIECE1 * first[s][1] + PIECE2 * part, PIECE2)].astype(F32)
            for k in range(3 * s, 3 * s + 3):
                total = total + got_b[e, k].astype(F32)
            sum_b[s, pl.ds(PIECE2 * part, PIECE2)] = total.astype(BF16)
            if e > 0:
                k = 3 * s + e - 1
                copy = remote(sum_b.at[s, pl.ds(PIECE2 * part, PIECE2)], got_c.at[k], c_send.at[k], c_recv.at[k], peer(e))
                copy.start()
                copies_c.append(copy)
    for copy in loss_b:
        copy.wait_recv()
    loss_y[y] = (loss_x[0] + loss_x[1]) + (loss_x[2] + loss_x[3])
    loss_c = [remote(loss_y.at[y], loss_y.at[y], l_send.at[3 + d], l_recv.at[3 + d], y_peer(d)) for d in (1, 2, 3)]
    for copy in loss_c:
        copy.start()
    for copy in copies_c + loss_c:
        copy.wait_recv()
    loss_z[z] = (loss_y[0] + loss_y[1]) + (loss_y[2] + loss_y[3])
    for s in range(2):
        total = sum_b[s, pl.ds(PIECE2 * second[s][1], PIECE2)].astype(F32)
        for k in range(3 * s, 3 * s + 3):
            total = total + got_c[k].astype(F32)
        sum_c[pl.ds(PIECE2 * s, PIECE2)] = total.astype(BF16)
    sum_c[pl.ds(2 * PIECE2, 2)] = jnp.zeros((2, 16, 128), BF16)

    copies_d = []
    for d in range(1, 8):
        to = (z + d) % 8
        copies_d.append(remote(sum_c.at[pl.ds(PIECE3 * to, PIECE3)], got_d.at[d - 1], d_send.at[d - 1], d_recv.at[d - 1], z_peer(d)))
    loss_d = [remote(loss_z.at[z], loss_z.at[z], l_send.at[6 + d], l_recv.at[6 + d], z_peer(d)) for d in range(1, 8)]
    for copy in copies_d + loss_d:
        copy.start()
    send_back(BACK_1, BACK_2)
    for copy in copies_d + loss_d:
        copy.wait_recv()
    total = sum_c[pl.ds(PIECE3 * z, PIECE3)].astype(F32)
    for k in range(7):
        total = total + got_d[k].astype(F32)
    gat_d[pl.ds(PIECE3 * z, PIECE3)] = total.astype(BF16)
    sums = [loss_z[k] for k in range(8)]
    loss_all = ((sums[0] + sums[1]) + (sums[2] + sums[3])) + ((sums[4] + sums[5]) + (sums[6] + sums[7]))
    loss_ref[0] = jnp.max(loss_all) / (3.0 * ROWS * ROWS * 256)

    mine = gat_d.at[pl.ds(PIECE3 * z, PIECE3)]
    copies_e = [remote(mine, mine, e_send.at[d - 1], e_recv.at[d - 1], z_peer(d)) for d in range(1, 8)]
    for copy in copies_e:
        copy.start()
    finish_text(0)
    finish_text(1)
    for copy in copies_e:
        copy.wait_recv()
    send_back(BACK_2, BACKS)

    copies_g = []
    for s in range(2):
        peer, at_s = second[s]
        src = gat_d.at[pl.ds(PIECE2 * s, PIECE2)]
        dst = gat_c.at[s, pl.ds(PIECE2 * at_s, PIECE2)]
        for d in (1, 2, 3):
            k = 3 * s + d - 1
            copies_g.append(remote(src, dst, g_send.at[k], g_recv.at[k], peer(d)))
    for copy in copies_g:
        copy.start()
    for s in range(2):
        gat_c[s, pl.ds(PIECE2 * second[s][1], PIECE2)] = gat_d[pl.ds(PIECE2 * s, PIECE2)]
    for copy in copies_g:
        copy.wait_recv()

    copies_h = []
    for s in range(2):
        peer, at_s = first[s]
        dst = gat_b.at[s, pl.ds(PIECE1 * at_s, PIECE1)]
        for d in (1, 2, 3):
            k = 3 * s + d - 1
            copies_h.append(remote(gat_c.at[s], dst, h_send.at[k], h_recv.at[k], peer(d)))
    for copy in copies_h:
        copy.start()
    for s in range(2):
        gat_b[s, pl.ds(PIECE1 * first[s][1], PIECE1)] = gat_c[s]
    for copy in copies_h:
        copy.wait_recv()

    copy_i = remote(gat_b, gat_a, i_send, i_recv, near)
    copy_i.start()

    def write_head(src, which):
        for s in range(2):

            def body(r, carry, s=s):
                row = pl.ds(pl.multiple_of(which * (HALF // 9 * 16) + s * (STREAM // 9 * 16) + r * 16, 16), 16)
                for c in range(9):
                    gh[row, 128 * c : 128 * c + 128] = src[s, r * 9 + c]
                return carry

            lax.fori_loop(0, STREAM // 9, body, 0)

    write_head(gat_b, core)
    copy_i.wait_recv()
    write_head(gat_a, 1 - core)

    for i in range(2, CHUNKS):
        finish_text(i)

    send_ids_far.wait_send()
    send_ids_near.wait_send()
    for i in range(CHUNKS):
        forward(i).wait_send()
        near_part(i).wait_send()
    for i in range(BACKS):
        back(i).wait_send()
    for copy in [send_zt, copy_a, loss_a, copy_i] + copies_b + loss_b + copies_c + loss_c + copies_d + loss_d + copies_e + copies_g + copies_h:
        copy.wait_send()


def shards(image_emb, text_feat, text_head, pair_ids, row_weight):
    anywhere = pl.BlockSpec(memory_space=pl.ANY)
    vmem = pl.BlockSpec(memory_space=pltpu.VMEM)
    block = (ROWS, WIDTH)
    dma = pltpu.SemaphoreType.DMA
    unit = (16, 128)
    scratch = [
        pltpu.VMEM(block, BF16),
        pltpu.VMEM(block, BF16),
        pltpu.VMEM((WIDTH, WIDTH), BF16),
        pltpu.VMEM(block, BF16),
        pltpu.VMEM((ROWS, 1), F32),
        pltpu.VMEM(block, F32),
        pltpu.VMEM((ROWS, 1), F32),
        pltpu.VMEM(block, BF16),
        pltpu.VMEM(block, BF16),
        pltpu.VMEM(block, BF16),
        pltpu.VMEM(block, BF16),
        pltpu.VMEM((4, 128), jnp.int32),
        pltpu.VMEM((4, 128), jnp.int32),
        pltpu.VMEM(block, F32),
        pltpu.VMEM(block, F32),
        pltpu.VMEM(block, BF16),
        pltpu.VMEM(block, BF16),
        pltpu.VMEM(block, BF16),
        pltpu.VMEM(block, BF16),
        pltpu.VMEM(block, BF16),
        pltpu.VMEM(block, BF16),
        pltpu.VMEM((ROWS, ROWS), BF16),
        pltpu.VMEM((ROWS, ROWS), BF16),
        pltpu.VMEM((ROWS, ROWS), BF16),
        pltpu.VMEM((1, ROWS), F32),
        pltpu.VMEM((WIDTH, WIDTH), F32),
        pltpu.VMEM((UNITS,) + unit, BF16),
        pltpu.VMEM((HALF,) + unit, BF16),
        pltpu.VMEM((HALF + 16,) + unit, BF16),
        pltpu.VMEM((4, 6, PIECE2) + unit, BF16),
        pltpu.VMEM((2, PIECE1) + unit, BF16),
        pltpu.VMEM((6, PIECE2) + unit, BF16),
        pltpu.VMEM((8 * PIECE3,) + unit, BF16),
        pltpu.VMEM((7, PIECE3) + unit, BF16),
        pltpu.VMEM((8 * PIECE3,) + unit, BF16),
        pltpu.VMEM((2, PIECE1) + unit, BF16),
        pltpu.VMEM((2, 4 * PIECE1) + unit, BF16),
        pltpu.VMEM((2, 4 * PIECE1) + unit, BF16),
        pltpu.VMEM((2, 8, 128), F32),
        pltpu.VMEM((4, 8, 128), F32),
        pltpu.VMEM((4, 8, 128), F32),
        pltpu.VMEM((8, 8, 128), F32),
        dma((3,)),
        dma((CHUNKS,)), dma((CHUNKS,)),
        dma((2,)), dma((2,)),
        dma, dma,
        dma((CHUNKS,)), dma((CHUNKS,)),
        dma((BACKS,)), dma((BACKS,)),
        dma, dma,
        dma((4, 6)), dma((4, 6)),
        dma((6,)), dma((6,)),
        dma((7,)), dma((7,)),
        dma((7,)), dma((7,)),
        dma((6,)), dma((6,)),
        dma((6,)), dma((6,)),
        dma, dma,
        dma((14,)), dma((14,)),
        pltpu.SemaphoreType.REGULAR,
    ]
    outs = pl.pallas_call(
        kernel,
        out_shape=(
            jax.ShapeDtypeStruct((1,), F32),
            pltpu.VMEM(block, BF16),
            pltpu.VMEM(block, BF16),
            pltpu.VMEM((WIDTH, WIDTH), BF16),
        ),
        in_specs=[anywhere, anywhere, anywhere, vmem, vmem],
        out_specs=(pl.BlockSpec(memory_space=pltpu.SMEM), vmem, vmem, vmem),
        scratch_shapes=scratch,
        compiler_params=pltpu.CompilerParams(
            collective_id=0, has_side_effects=True, vmem_limit_bytes=50 * 1024 * 1024
        ),
        name="contrast",
    )(image_emb, text_feat, text_head, pair_ids.reshape(4, 128), row_weight)
    return tuple(outs)


def solution(mesh):
    in_specs = (P("dp", None), P("dp", None), P(), P("dp"), P("dp"))
    out_specs = (P(), P("dp", None), P("dp", None), P())
    return jax.shard_map(shards, mesh=mesh, in_specs=in_specs, out_specs=out_specs, check_vma=False)
```
